128 devices in a mesh: dp: 16 (over z_hi, x, core), tensor: 8 (over z_lo, y).
Axes of the slice: x: 4, y: 4, z: 4 (z_hi: 2, z_lo: 2; z = z_hi * 2 + z_lo), core: 2. Of those that a mesh axis runs over, the one named last changes fastest.
Arguments:
- hidden: bfloat16 [8192, 13824], P('dp', 'tensor'), may hold values from -6 to 6
- weight: bfloat16 [13824, 3072], P('tensor', 'dp'), may hold values from -0.0546875 to 0.0546875
- momentum: bfloat16 [16, 13824, 3072], P('dp', 'tensor'), may hold values from -6 to 6
- target: bfloat16 [8192, 3072], P('dp', 'tensor'), may hold values from -6 to 6
- freqs: int32 [48, 8], replicated, may hold values from 0 to 63, as said below
Outputs:
- new_momentum: bfloat16 [16, 13824, 3072], P('dp', 'tensor')
- update: float32 [13824, 3072], P('tensor', 'dp')
The draws below stay inside these ranges and needn't reach their ends.
Inputs may be any that keep to these rules, and one draw needn't show every extreme that they name: `freqs`: the 8 frequencies of a block are distinct; every block holds 0 and 63.
All inputs are finite; a program needn't handle non-finite values.
Results may differ from the reference program's by a relative error of at most 0.017.
Values may be sent and summed in bfloat16 or wider, within the bound.
No kernel may reach another device: no remote copies, remote signals or barrier semaphores. Data moves between devices by JAX's collectives and lax.ppermute only.
A program may use at most 192 MiB of HBM per device.

```python
import math
import jax
import jax.numpy as jnp
from jax import lax

D = 3072
FF = 13824
CL = 64
KEEP = 8
TOK_DEV = 512
REPLICAS = 16
TOKENS = 8192
BLOCKS = 48


def draw_freqs(key, part):
    key = jax.random.fold_in(key, 7)
    subkeys = jax.random.split(key, BLOCKS)

    def single(sub_key):
        middle = jax.random.permutation(sub_key, CL - 2)[:KEEP - 2] + 1
        return jnp.concatenate([jnp.zeros((1,), jnp.int32), middle.astype(jnp.int32), jnp.full((1,), CL - 1, jnp.int32)])
    return jax.vmap(single)(subkeys).astype(jnp.int32)


def raised(result, stream_key, source, target, parts, factor):
    owner, partner = [(jnp.arange(result.shape[axis_at]) // (result.shape[axis_at] // parts)).reshape([-1 if axis == axis_at else 1 for axis in range(result.ndim)]) for axis_at in (source, target)]
    chosen = jax.random.permutation(stream_key, parts)[partner]
    strong = (owner == chosen) | (owner == (partner + parts // 2) % parts)
    return jnp.where(strong, factor * result, result)


def steps_of(key, extent, cuts, smallest, high):
    gain, own = 1.0, jax.random.fold_in(key, 6)
    for dim, blocks in cuts:
        heights = jnp.exp(jax.random.uniform(jax.random.fold_in(own, dim), (blocks,), jnp.float32, smallest / len(cuts), high / len(cuts)))
        gain = gain * jnp.repeat(heights, extent[dim] // blocks).reshape([-1 if axis == dim else 1 for axis in range(len(extent))])
    return gain


def normal_values(stream_key, dims, scale, reach, pieces=(), held_as=jnp.bfloat16):
    array = jax.random.normal(stream_key, dims, jnp.float32) * scale
    if len(pieces) > 0:
        array = steps_of(stream_key, dims, pieces, -0.22, 0.18) * array
    return jnp.clip(array, min=-reach, max=reach).astype(held_as)


def bell_draw_with(stream_key, shape, scale, bound, pieces, heavy, held_as=jnp.bfloat16):
    array = scale * jax.random.normal(stream_key, shape, jnp.float32)
    if pieces:
        array = array * steps_of(stream_key, shape, pieces, -0.22, 0.18)
    return jnp.clip(raised(array, jax.random.fold_in(stream_key, 3), *heavy), -bound, bound).astype(held_as)


def setup_inputs(seed: int = 0) -> dict:
    key_of = jax.random.split(jax.random.key(seed), 6)
    return {
        "hidden": normal_values(key_of[0], (TOKENS, FF), 1.0, 6.0, ((0, 16), (1, 8))),
        "weight": normal_values(key_of[1], (FF, D), FF ** -0.5, 0.0546875, ((0, 8), (1, 16))),
        "momentum": bell_draw_with(key_of[2], (REPLICAS, FF, D), 1.0, 6.0, ((0, 16), (1, 8)), (0, 2, 16, 2.0)),
        "target": normal_values(key_of[3], (TOKENS, D), 1.0, 6.0, ((0, 16), (1, 8))),
        "freqs": draw_freqs(jax.random.fold_in(key_of[5], 71), 0),
    }


decay_rate = 0.9

def cosine_table():
    freq_ids = jnp.arange(CL, dtype=jnp.float32)[:, None]
    cell_ids = jnp.arange(CL, dtype=jnp.float32)[None, :]
    scale_row = jnp.where(freq_ids == 0, math.sqrt(1.0 / CL), math.sqrt(2.0 / CL))
    return scale_row * jnp.cos(math.pi * (2.0 * cell_ids + 1.0) * freq_ids / (2.0 * CL))

def reference(hidden, weight, momentum, target, freqs):
    highest_mode = lax.Precision.HIGHEST
    chosen = cosine_table()[freqs]
    factor = 1.0 / math.sqrt(TOK_DEV)

    def replica(carry, inputs):
        hid_rows, old_state, goal_rows = inputs
        output = jnp.dot(hid_rows, weight, preferred_element_type=jnp.float32)
        residual = (output - goal_rows.astype(jnp.float32)).astype(jnp.bfloat16)
        gradient = jnp.dot(hid_rows.T, residual, preferred_element_type=jnp.float32) * factor
        primed = decay_rate * old_state.astype(jnp.float32) + gradient
        grouped = primed.reshape(FF, BLOCKS, CL)
        coeffs = jnp.einsum('fcj,ckj->fck', grouped, chosen, precision=highest_mode)
        kept_part = grouped - jnp.einsum('fck,ckj->fcj', coeffs, chosen, precision=highest_mode)
        return (carry + coeffs, kept_part.reshape(FF, D).astype(jnp.bfloat16))
    start_sum = jnp.zeros((FF, BLOCKS, KEEP), jnp.float32)
    total, new_state = lax.scan(replica, start_sum, (hidden.reshape(REPLICAS, TOK_DEV, FF), momentum, target.reshape(REPLICAS, TOK_DEV, D)))
    update = jnp.einsum('fck,ckj->fcj', total, chosen, precision=highest_mode).reshape(FF, D) / REPLICAS
    return (new_state, update)
```

```python
import functools
import math

import jax
import jax.numpy as jnp
from jax import lax
from jax.experimental import pallas as pl
from jax.experimental.pallas import tpu as pltpu
from jax.sharding import Mesh, PartitionSpec as P
import numpy as np

CL = 64
DECAY = 0.9
AXES = ("zh", "x", "c", "zl", "y")
DP = ("zh", "x", "c")
TENSOR = ("zl", "y")
CHUNKS = (((0, 0), (1, 0), (0, 1), (0, 3), (0, 2), (1, 1), (1, 3), (1, 2)),)


def cosine_table():
    freq_ids = jnp.arange(CL, dtype=jnp.float32)[:, None]
    cell_ids = jnp.arange(CL, dtype=jnp.float32)[None, :]
    scale_row = jnp.where(freq_ids == 0, math.sqrt(1.0 / CL), math.sqrt(2.0 / CL))
    return scale_row * jnp.cos(math.pi * (2.0 * cell_ids + 1.0) * freq_ids / (2.0 * CL))


def shift(sizes, **by):
    step = [by.get(a, 0) for a in AXES]
    pairs = []
    for at in np.ndindex(*sizes):
        to = [(a + s) % n for a, s, n in zip(at, step, sizes)]
        pairs.append((int(np.ravel_multi_index(at, sizes)), int(np.ravel_multi_index(to, sizes))))
    return pairs


def output_kernel(n, info, ht_ref, target_ref, *refs):
    out_ref = refs[-1]
    core = info[0]
    half = refs[0].shape[0]
    for u in range(n):
        for which in range(2):
            w_ref = refs[2 * u + which]
            slot = core if which == 0 else 1 - core
            value = jnp.dot(w_ref[...], ht_ref[...], preferred_element_type=jnp.float32)
            rows = pl.ds(pl.multiple_of((2 * u + slot) * half, half), half)
            out_ref[rows, :] = value.astype(jnp.bfloat16)

        @pl.when(info[1 + u] != 0)
        def _():
            rows = pl.ds(2 * u * half, 2 * half)
            goal = target_ref[...].astype(jnp.float32).T
            out_ref[rows, :] = (out_ref[rows, :].astype(jnp.float32) - goal).astype(jnp.bfloat16)


def partial_output(info, ht, target, blocks):
    n = len(blocks) // 2
    half, depth = blocks[0].shape
    tokens = ht.shape[1]
    vmem = pl.BlockSpec(memory_space=pltpu.VMEM)
    return pl.pallas_call(
        functools.partial(output_kernel, n),
        out_shape=jax.ShapeDtypeStruct((2 * n * half, tokens), jnp.bfloat16),
        in_specs=[pl.BlockSpec(memory_space=pltpu.SMEM)] + [vmem] * (2 + len(blocks)),
        out_specs=vmem,
        compiler_params=pltpu.CompilerParams(vmem_limit_bytes=48 * 2**20),
        cost_estimate=pl.CostEstimate(
            flops=4 * n * half * depth * tokens,
            bytes_accessed=2 * (2 * n * half * (depth + tokens) + depth * tokens),
            transcendentals=0,
        ),
    )(info, ht, target, *blocks)


def step_kernel(factor, first, info, ht_ref, rt_ref, m_ref, keep_ref, code_ref, *refs):
    new_ref, mine_ref, other_ref = refs[-3:]
    rows = m_ref.shape[0]
    width = m_ref.shape[1]
    mine = mine_ref.shape[0]
    rt = rt_ref[...]
    keep = keep_ref[0]
    code = code_ref[0]
    for start in range(0, rows, 512):
        size = min(512, rows - start)
        f = pl.ds(start, size)
        grad = lax.dot_general(
            ht_ref[f, :], rt, (((1,), (1,)), ((), ())), preferred_element_type=jnp.float32
        )
        primed = DECAY * m_ref[f, :].astype(jnp.float32) + grad * factor
        low = primed.astype(jnp.bfloat16)
        for a in range(0, width, 256):
            b = min(a + 256, width)
            gone = jnp.dot(low[:, a:b], keep[a:b, a:b], preferred_element_type=jnp.float32)
            new_ref[f, a:b] = (primed[:, a:b] - gone).astype(jnp.bfloat16)
        coeffs = lax.dot_general(
            code, low, (((1,), (1,)), ((), ())), preferred_element_type=jnp.float32
        ).astype(jnp.bfloat16)
        mine_ref[:, f] = coeffs[:mine]
        other_ref[:, f] = coeffs[mine:]


def momentum_step(chips, ht, rt, momentum, keep, code, state, factor):
    n = chips.shape[0]
    rows, width_all = momentum.shape
    tokens = ht.shape[1]
    width = rt.shape[0] // n
    kept = code.shape[1]
    mine = kept // 2
    in_specs = [
        pl.BlockSpec((rows, tokens), lambda u, c: (0, 0)),
        pl.BlockSpec((width, tokens), lambda u, c: (u, 0)),
        pl.BlockSpec((rows, width), lambda u, c: (0, c[u])),
        pl.BlockSpec((1, width, width), lambda u, c: (c[u], 0, 0)),
        pl.BlockSpec((1, kept, width), lambda u, c: (c[u], 0, 0)),
    ]
    args = [ht, rt, momentum, keep, code]
    alias = {}
    if state is not None:
        in_specs.append(pl.BlockSpec(memory_space=pl.ANY))
        args.append(state)
        alias = {6: 0}
    return pl.pallas_call(
        functools.partial(step_kernel, factor, state is None),
        out_shape=(
            jax.ShapeDtypeStruct((rows, width_all), jnp.bfloat16),
            jax.ShapeDtypeStruct((n, mine, rows), jnp.bfloat16),
            jax.ShapeDtypeStruct((n, mine, rows), jnp.bfloat16),
        ),
        grid_spec=pltpu.PrefetchScalarGridSpec(
            num_scalar_prefetch=1,
            grid=(n,),
            in_specs=in_specs,
            out_specs=(
                pl.BlockSpec((rows, width), lambda u, c: (0, c[u])),
                pl.BlockSpec((None, mine, rows), lambda u, c: (u, 0, 0)),
                pl.BlockSpec((None, mine, rows), lambda u, c: (u, 0, 0)),
            ),
        ),
        input_output_aliases=alias,
        compiler_params=pltpu.CompilerParams(
            vmem_limit_bytes=48 * 2**20, dimension_semantics=("arbitrary",)
        ),
        cost_estimate=pl.CostEstimate(
            flops=2 * n * rows * width * (tokens + 256 + kept),
            bytes_accessed=2 * (2 * n * rows * width + rows * tokens),
            transcendentals=0,
        ),
    )(chips, *args)


def tables(freqs, core, n_chips):
    onehot = (freqs[:, :, None] == jnp.arange(CL, dtype=jnp.int32)[None, None, :]).astype(jnp.float32)
    chosen = jnp.einsum("ckv,vj->ckj", onehot, cosine_table(), precision=lax.Precision.HIGHEST)
    blocks, kept, _ = chosen.shape
    per = blocks // n_chips
    same = jnp.eye(per, dtype=jnp.float32)
    proj = jnp.einsum("ckj,ckl->cjl", chosen, chosen, precision=lax.Precision.HIGHEST)
    proj = proj.reshape(n_chips, per, CL, 1, CL) * same[None, :, None, :, None]
    keep = proj.reshape(n_chips, per * CL, per * CL).astype(jnp.bfloat16)
    code = chosen.reshape(n_chips, per, kept, 1, CL) * same[None, :, None, :, None]
    code = code.reshape(n_chips, 2, per * kept // 2, per * CL)
    code = jnp.where(core == 0, code, code[:, ::-1]).reshape(n_chips, per * kept, per * CL)
    return chosen, keep, code.astype(jnp.bfloat16)


def per_device(sizes, hidden, weight, momentum, target, freqs):
    send = lambda v, **by: lax.ppermute(v, AXES, shift(sizes, **by))
    zh, x, c = (lax.axis_index(a) for a in DP)
    n_zh, n_x = sizes[0], sizes[1]
    n_tensor = sizes[3] * sizes[4]
    shard = lax.axis_index(TENSOR)
    chip_at = lambda s: ((zh + s[0]) % n_zh) * n_x + (x + s[1]) % n_x

    ht = hidden.T
    own = weight.T
    factor = 1.0 / math.sqrt(hidden.shape[0])

    blocks = {(0, 0): own}
    blocks[1, 0] = send(own, zh=1)
    blocks[0, 1] = send(own, x=-1)
    blocks[0, 3] = send(own, x=1)
    blocks[0, 2] = send(own, x=2)
    blocks[1, 1] = send(blocks[1, 0], x=-1)
    blocks[1, 3] = send(blocks[1, 0], x=1)
    blocks[1, 2] = send(blocks[0, 2], zh=1)
    swapped = {s: send(b, c=1) for s, b in blocks.items()}

    chosen, keep, code = tables(freqs, c, n_zh * n_x)

    state = None
    parts = []
    for chunk in CHUNKS:
        n = len(chunk)
        chips = jnp.stack([chip_at(s) for s in chunk]).astype(jnp.int32)
        info = jnp.concatenate([c[None].astype(jnp.int32), (chips == shard).astype(jnp.int32)])
        pairs = [b for s in chunk for b in (blocks[s], swapped[s])]
        partial = partial_output(info, ht, target, pairs)
        split = partial.reshape(n_tensor, partial.shape[0] // n_tensor, partial.shape[1])
        received = lax.all_to_all(split, TENSOR, 0, 0)
        residual = jnp.sum(received.astype(jnp.float32), axis=0).astype(jnp.bfloat16)
        gathered = lax.all_gather(residual, TENSOR, axis=0, tiled=True)
        state, mine, other = momentum_step(chips, ht, gathered, momentum[0], keep, code, state, factor)
        pair = (mine.astype(jnp.float32) + send(other, c=1).astype(jnp.float32)).astype(jnp.bfloat16)
        for u, s in enumerate(chunk):
            parts.append(pair[u] if s == (0, 0) else send(pair[u], zh=s[0], x=s[1]))

    total = sum(p.astype(jnp.float32) for p in parts)
    per = chosen.shape[0] // (n_zh * n_x * sizes[2])
    own_basis = lax.dynamic_slice_in_dim(chosen, lax.axis_index(DP) * per, per, 0)
    decoded = jnp.einsum(
        "ckf,ckj->cjf",
        total.reshape(per, total.shape[0] // per, total.shape[1]),
        own_basis * (1.0 / (n_zh * n_x * sizes[2])),
        precision=lax.Precision.HIGHEST,
    )
    return state[None], decoded.reshape(per * CL, -1).T


def solution(mesh):
    sizes = (2, 4, 2, 2, 4)
    fine = Mesh(mesh.devices.reshape(sizes), AXES)
    in_specs = (P(DP, TENSOR), P(TENSOR, DP), P(DP, TENSOR, None), P(DP, TENSOR), P())
    out_specs = (P(DP, TENSOR, None), P(TENSOR, DP))
    return jax.shard_map(
        functools.partial(per_device, sizes),
        mesh=fine,
        in_specs=in_specs,
        out_specs=out_specs,
        check_vma=False,
    )
```

```python
import functools
import math

import jax
import jax.numpy as jnp
from jax import lax
from jax.experimental import pallas as pl
from jax.experimental.pallas import tpu as pltpu
from jax.sharding import Mesh, PartitionSpec as P
import numpy as np

CL = 64
DECAY = 0.9
AXES = ("zh", "x", "c", "zl", "y")
DP = ("zh", "x", "c")
TENSOR = ("zl", "y")
ANY = pl.BlockSpec(memory_space=pl.ANY)
CHUNK_US = (4, 6)
TILE = 896
CHUNKS = (((0, 0), (1, 0), (0, 1), (0, 3)), ((0, 2), (1, 1), (1, 3), (1, 2)))


def cosine_table():
    freq_ids = jnp.arange(CL, dtype=jnp.float32)[:, None]
    cell_ids = jnp.arange(CL, dtype=jnp.float32)[None, :]
    scale_row = jnp.where(freq_ids == 0, math.sqrt(1.0 / CL), math.sqrt(2.0 / CL))
    return scale_row * jnp.cos(math.pi * (2.0 * cell_ids + 1.0) * freq_ids / (2.0 * CL))


def shift(sizes, **by):
    step = [by.get(a, 0) for a in AXES]
    pairs = []
    for at in np.ndindex(*sizes):
        to = [(a + s) % n for a, s, n in zip(at, step, sizes)]
        pairs.append((int(np.ravel_multi_index(at, sizes)), int(np.ravel_multi_index(to, sizes))))
    return pairs


def output_kernel(pieces, info, ht_ref, target_ref, *refs):
    blocks, (out_ref, w_ref, sems) = refs[:-3], refs[-3:]
    core = info[0]
    shards, n, rows, _ = out_ref.shape
    half = shards * rows // 2
    copies = []
    at = 0
    for k, count in enumerate(pieces):
        slot = core if k % 2 == 0 else 1 - core
        base = (k // 2 * 2 + slot) * half
        for _ in range(count):
            size = blocks[at].shape[0]
            to = pl.ds(pl.multiple_of(base, 16), size)
            copies.append((k // 2, pltpu.make_async_copy(blocks[at], w_ref.at[to], sems.at[at])))
            base = base + size
            at += 1
    for _, copy in copies:
        copy.start()
    for u in range(n):
        for unit, copy in copies:
            if unit == u:
                copy.wait()
        value = jnp.dot(
            w_ref[2 * u * half : 2 * (u + 1) * half], ht_ref[...], preferred_element_type=jnp.float32
        )
        for i in range(shards):
            out_ref[i, u] = value[i * rows : (i + 1) * rows].astype(jnp.bfloat16)

        @pl.when(info[1 + u] != 0)
        def _():
            goal = target_ref[...].astype(jnp.float32).T
            for i in range(shards):
                here = out_ref[i, u].astype(jnp.float32) - goal[i * rows : (i + 1) * rows]
                out_ref[i, u] = here.astype(jnp.bfloat16)


def partial_output(shards, info, ht, target, blocks, us):
    depth, count = ht.shape
    width = target.shape[1]
    n = len(blocks) // 2
    pieces = tuple(len(b) for b in blocks)
    blocks = [piece for b in blocks for piece in b]
    vmem = pl.BlockSpec(memory_space=pltpu.VMEM)
    return pl.pallas_call(
        functools.partial(output_kernel, pieces),
        out_shape=jax.ShapeDtypeStruct((shards, n, width // shards, count), jnp.bfloat16),
        in_specs=[pl.BlockSpec(memory_space=pltpu.SMEM), vmem, vmem] + [ANY] * len(blocks),
        out_specs=vmem,
        scratch_shapes=[
            pltpu.VMEM((n * width, depth), jnp.bfloat16),
            pltpu.SemaphoreType.DMA((len(blocks),)),
        ],
        compiler_params=pltpu.CompilerParams(vmem_limit_bytes=56 * 2**20),
        cost_estimate=pl.CostEstimate(flops=int(us * 10**9), bytes_accessed=1, transcendentals=0),
    )(info, ht, target, *blocks)


def residual_kernel(parts_ref, *refs):
    out_ref = refs[-1]
    for u in range(out_ref.shape[1]):
        total = jnp.sum(parts_ref[:, u].astype(jnp.float32), axis=0).astype(jnp.bfloat16)
        for k in range(out_ref.shape[0]):
            out_ref[k, u] = total


def residual_copies(parts, after):
    vmem = pl.BlockSpec(memory_space=pltpu.VMEM)
    return pl.pallas_call(
        residual_kernel,
        out_shape=jax.ShapeDtypeStruct(parts.shape, jnp.bfloat16),
        in_specs=[vmem] + [ANY] * len(after),
        out_specs=vmem,
        compiler_params=pltpu.CompilerParams(vmem_limit_bytes=48 * 2**20),
        cost_estimate=pl.CostEstimate(flops=parts.size, bytes_accessed=4 * parts.size, transcendentals=0),
    )(parts, *after)


def step_kernel(factor, info, ht_ref, rt_ref, m_ref, keep_ref, code_ref, *refs):
    new_ref, mine_ref, other_ref = refs[-3:]
    rows = m_ref.shape[0]
    width = m_ref.shape[1]
    mine = mine_ref.shape[0]
    rt = rt_ref[...].reshape(width, rt_ref.shape[2])
    keep = keep_ref[0]
    code = code_ref[0]
    for start in range(0, rows, TILE):
        size = min(TILE, rows - start)
        f = pl.ds(start, size)
        grad = lax.dot_general(
            ht_ref[f, :], rt, (((1,), (1,)), ((), ())), preferred_element_type=jnp.float32
        )
        primed = DECAY * m_ref[f, :].astype(jnp.float32) + grad * factor
        low = primed.astype(jnp.bfloat16)
        for a in range(0, width, 256):
            b = min(a + 256, width)
            gone = jnp.dot(low[:, a:b], keep[a:b, a:b], preferred_element_type=jnp.float32)
            new_ref[f, a:b] = (primed[:, a:b] - gone).astype(jnp.bfloat16)
        coeffs = lax.dot_general(
            code, low, (((1,), (1,)), ((), ())), preferred_element_type=jnp.float32
        ).astype(jnp.bfloat16)
        mine_ref[:, f] = coeffs[:mine]
        other_ref[:, f] = coeffs[mine:]


def momentum_step(chips, ht, rt, momentum, keep, code, state, factor):
    n = chips.shape[0]
    n_chips = code.shape[0]
    rows, width_all = momentum.shape
    tokens = ht.shape[1]
    shards, _, slab, _ = rt.shape
    width = shards * slab
    kept = code.shape[1]
    mine = kept // 2
    in_specs = [
        pl.BlockSpec((rows, tokens), lambda u, c: (0, 0)),
        pl.BlockSpec((shards, None, slab, tokens), lambda u, c: (0, u, 0, 0)),
        pl.BlockSpec((rows, width), lambda u, c: (0, c[u])),
        pl.BlockSpec((1, width, width), lambda u, c: (c[u], 0, 0)),
        pl.BlockSpec((1, kept, width), lambda u, c: (c[u], 0, 0)),
    ]
    args = [ht, rt, momentum, keep, code]
    alias = {}
    if state is not None:
        in_specs += [ANY] * 3
        args += state
        alias = {6: 0, 7: 1, 8: 2}
    return pl.pallas_call(
        functools.partial(step_kernel, factor),
        out_shape=(
            jax.ShapeDtypeStruct((rows, width_all), jnp.bfloat16),
            jax.ShapeDtypeStruct((n_chips, mine, rows), jnp.bfloat16),
            jax.ShapeDtypeStruct((n_chips, mine, rows), jnp.bfloat16),
        ),
        grid_spec=pltpu.PrefetchScalarGridSpec(
            num_scalar_prefetch=1,
            grid=(n,),
            in_specs=in_specs,
            out_specs=(
                pl.BlockSpec((rows, width), lambda u, c: (0, c[u])),
                pl.BlockSpec((None, mine, rows), lambda u, c: (c[u], 0, 0)),
                pl.BlockSpec((None, mine, rows), lambda u, c: (c[u], 0, 0)),
            ),
        ),
        input_output_aliases=alias,
        compiler_params=pltpu.CompilerParams(
            vmem_limit_bytes=60 * 2**20, dimension_semantics=("arbitrary",)
        ),
        cost_estimate=pl.CostEstimate(
            flops=2 * n * rows * width * (tokens + 256 + kept),
            bytes_accessed=2 * (2 * n * rows * width + rows * tokens),
            transcendentals=0,
        ),
    )(chips, *args)


def table_kernel(info, freqs_ref, cosines_ref, keep_ref, code_ref):
    rows, width = code_ref.shape[1:]
    per = width // CL
    kept = rows // per
    freqs = freqs_ref[0]
    onehot = (freqs == lax.broadcasted_iota(jnp.int32, (rows, CL), 1)).astype(jnp.float32)
    chosen = jnp.dot(
        onehot, cosines_ref[...], precision=lax.Precision.HIGHEST, preferred_element_type=jnp.float32
    )
    wide = jnp.concatenate([chosen] * per, axis=1)
    block = lax.broadcasted_iota(jnp.int32, (rows, width), 0) // kept + info[0] * (per // 2)
    block = jnp.where(block >= per, block - per, block)
    wide = jnp.where(block == lax.broadcasted_iota(jnp.int32, (rows, width), 1) // CL, wide, 0.0)
    code_ref[0] = wide.astype(jnp.bfloat16)
    keep_ref[...] = jnp.zeros(keep_ref.shape, jnp.bfloat16)
    for a in range(0, width, 128):
        tile = wide[:, a : a + 128]
        keep_ref[0, a : a + 128, a : a + 128] = lax.dot_general(
            tile,
            tile,
            (((0,), (0,)), ((), ())),
            precision=lax.Precision.HIGHEST,
            preferred_element_type=jnp.float32,
        ).astype(jnp.bfloat16)


def tables(freqs, core, n_chips):
    blocks, kept = freqs.shape
    per = blocks // n_chips
    ordered = freqs.reshape(n_chips, 2, per // 2 * kept)
    ordered = jnp.where(core == 0, ordered, ordered[:, ::-1]).reshape(n_chips, per * kept, 1)
    return pl.pallas_call(
        table_kernel,
        out_shape=(
            jax.ShapeDtypeStruct((n_chips, per * CL, per * CL), jnp.bfloat16),
            jax.ShapeDtypeStruct((n_chips, per * kept, per * CL), jnp.bfloat16),
        ),
        grid=(n_chips,),
        in_specs=[
            pl.BlockSpec(memory_space=pltpu.SMEM),
            pl.BlockSpec((1, per * kept, 1), lambda u: (u, 0, 0)),
            pl.BlockSpec((CL, CL), lambda u: (0, 0)),
        ],
        out_specs=(
            pl.BlockSpec((1, per * CL, per * CL), lambda u: (u, 0, 0)),
            pl.BlockSpec((1, per * kept, per * CL), lambda u: (u, 0, 0)),
        ),
        compiler_params=pltpu.CompilerParams(vmem_limit_bytes=32 * 2**20),
        cost_estimate=pl.CostEstimate(flops=10**9, bytes_accessed=4 * 10**6, transcendentals=0),
    )(core[None].astype(jnp.int32), ordered, cosine_table())


def per_device(sizes, hidden, weight, momentum, target, freqs):
    send = lambda v, **by: lax.ppermute(v, AXES, shift(sizes, **by))
    zh, x, c = (lax.axis_index(a) for a in DP)
    n_zh, n_x = sizes[0], sizes[1]
    n_tensor = sizes[3] * sizes[4]
    shard = lax.axis_index(TENSOR)
    n_chips = n_zh * n_x
    ht = hidden.T
    own = weight.T
    factor = 1.0 / math.sqrt(hidden.shape[0])

    cut = own.shape[0] // 2
    blocks = {(0, 0): [own], (1, 0): [send(own, zh=1)], (0, 1): [send(own, x=-1)], (0, 3): [send(own, x=1)]}
    for z in range(2):
        if z:
            blocks[z, 1] = [send(blocks[z, 0][0], x=-1)]
            blocks[z, 3] = [send(blocks[z, 0][0], x=1)]
        blocks[z, 2] = [send(blocks[z, 1][0][:cut], x=-1), send(blocks[z, 3][0][cut:], x=1)]
    swapped = {s: [send(piece, c=1) for piece in b] for s, b in blocks.items()}
    keep, code = tables(freqs, c, n_chips)

    core = c[None].astype(jnp.int32)
    chips, partials = [], []
    for chunk, us in zip(CHUNKS, CHUNK_US):
        at = jnp.stack([((zh + s[0]) % n_zh) * n_x + (x + s[1]) % n_x for s in chunk]).astype(jnp.int32)
        chips.append(at)
        partials.append(
            partial_output(
                n_tensor,
                jnp.concatenate([core, (at == shard).astype(jnp.int32)]),
                ht,
                target,
                [b for s in chunk for b in (blocks[s], swapped[s])],
                us,
            )
        )
    received = [lax.all_to_all(p, TENSOR, 0, 0) for p in partials]
    copies = [residual_copies(r, partials[i + 1 :]) for i, r in enumerate(received)]
    gathered = [lax.all_to_all(k, TENSOR, 0, 0) for k in copies]

    state = None
    for at, whole in zip(chips, gathered):
        state = momentum_step(at, ht, whole, momentum[0], keep, code, state, factor)
    state, mine, other = state

    pair = (mine.astype(jnp.float32) + send(other, c=1).astype(jnp.float32)).astype(jnp.bfloat16)
    total = jnp.sum(lax.all_to_all(pair, ("zh", "x"), 0, 0).astype(jnp.float32), axis=0)
    n_dp = n_chips * sizes[2]
    per = freqs.shape[0] // n_dp
    own_freqs = lax.dynamic_slice_in_dim(freqs, lax.axis_index(DP) * per, per, 0)
    onehot = (own_freqs[:, :, None] == jnp.arange(CL, dtype=jnp.int32)).astype(jnp.float32)
    own_basis = jnp.einsum("ckv,vj->ckj", onehot, cosine_table(), precision=lax.Precision.HIGHEST)
    decoded = jnp.einsum(
        "ckf,ckj->cjf",
        total.reshape(per, total.shape[0] // per, total.shape[1]),
        own_basis * (1.0 / n_dp),
        precision=lax.Precision.HIGHEST,
    )
    return state[None], decoded.reshape(per * CL, -1).T


def solution(mesh):
    sizes = (2, 4, 2, 2, 4)
    fine = Mesh(mesh.devices.reshape(sizes), AXES)
    in_specs = (P(DP, TENSOR), P(TENSOR, DP), P(DP, TENSOR, None), P(DP, TENSOR), P())
    out_specs = (P(DP, TENSOR, None), P(TENSOR, DP))
    return jax.shard_map(
        functools.partial(per_device, sizes),
        mesh=fine,
        in_specs=in_specs,
        out_specs=out_specs,
        check_vma=False,
    )
```

```python
import functools
import math

import jax
import jax.numpy as jnp
from jax import lax
from jax.experimental import pallas as pl
from jax.experimental.pallas import tpu as pltpu
from jax.sharding import Mesh, PartitionSpec as P
import numpy as np

CL = 64
DECAY = 0.9
AXES = ("zh", "x", "c", "zl", "y")
DP = ("zh", "x", "c")
TENSOR = ("zl", "y")
ANY = pl.BlockSpec(memory_space=pl.ANY)
TILE = 896
CHUNKS = (((0, 0), (1, 0), (0, 1), (0, 3)), ((0, 2), (1, 1), (1, 3), (1, 2)))
CHUNK_US = (4, 6)
MARK_US = 6


def cosine_table():
    freq_ids = jnp.arange(CL, dtype=jnp.float32)[:, None]
    cell_ids = jnp.arange(CL, dtype=jnp.float32)[None, :]
    scale_row = jnp.where(freq_ids == 0, math.sqrt(1.0 / CL), math.sqrt(2.0 / CL))
    return scale_row * jnp.cos(math.pi * (2.0 * cell_ids + 1.0) * freq_ids / (2.0 * CL))


def shift(sizes, **by):
    step = [by.get(a, 0) for a in AXES]
    pairs = []
    for at in np.ndindex(*sizes):
        to = [(a + s) % n for a, s, n in zip(at, step, sizes)]
        pairs.append((int(np.ravel_multi_index(at, sizes)), int(np.ravel_multi_index(to, sizes))))
    return pairs


def output_kernel(pieces, info, ht_ref, target_ref, *refs):
    blocks, (out_ref, w_ref, sems) = refs[: sum(pieces)], refs[-3:]
    core = info[0]
    shards, n, rows, _ = out_ref.shape
    half = shards * rows // 2
    copies = []
    at = 0
    for k, count in enumerate(pieces):
        slot = core if k % 2 == 0 else 1 - core
        base = (k // 2 * 2 + slot) * half
        for _ in range(count):
            size = blocks[at].shape[0]
            to = pl.ds(pl.multiple_of(base, 16), size)
            copies.append((k // 2, pltpu.make_async_copy(blocks[at], w_ref.at[to], sems.at[at])))
            base = base + size
            at += 1
    for _, copy in copies:
        copy.start()
    for u in range(n):
        for unit, copy in copies:
            if unit == u:
                copy.wait()
        value = jnp.dot(
            w_ref[2 * u * half : 2 * (u + 1) * half], ht_ref[...], preferred_element_type=jnp.float32
        )
        for i in range(shards):
            out_ref[i, u] = value[i * rows : (i + 1) * rows].astype(jnp.bfloat16)

        @pl.when(info[1 + u] != 0)
        def _():
            goal = target_ref[...].astype(jnp.float32).T
            for i in range(shards):
                here = out_ref[i, u].astype(jnp.float32) - goal[i * rows : (i + 1) * rows]
                out_ref[i, u] = here.astype(jnp.bfloat16)


def partial_output(shards, info, ht, target, blocks, us):
    depth, count = ht.shape
    width = target.shape[1]
    n = len(blocks) // 2
    pieces = tuple(len(b) for b in blocks)
    blocks = [piece for b in blocks for piece in b]
    vmem = pl.BlockSpec(memory_space=pltpu.VMEM)
    return pl.pallas_call(
        functools.partial(output_kernel, pieces),
        out_shape=jax.ShapeDtypeStruct((shards, n, width // shards, count), jnp.bfloat16),
        in_specs=[pl.BlockSpec(memory_space=pltpu.SMEM), vmem, vmem] + [ANY] * len(blocks),
        out_specs=vmem,
        scratch_shapes=[
            pltpu.VMEM((n * width, depth), jnp.bfloat16),
            pltpu.SemaphoreType.DMA((len(blocks),)),
        ],
        compiler_params=pltpu.CompilerParams(vmem_limit_bytes=56 * 2**20),
        cost_estimate=pl.CostEstimate(flops=int(us * 10**9), bytes_accessed=1, transcendentals=0),
    )(info, ht, target, *blocks)


def residual_kernel(parts_ref, *refs):
    out_ref = refs[-1]
    for u in range(out_ref.shape[1]):
        total = jnp.sum(parts_ref[:, u].astype(jnp.float32), axis=0).astype(jnp.bfloat16)
        for k in range(out_ref.shape[0]):
            out_ref[k, u] = total


def residual_copies(parts, after):
    vmem = pl.BlockSpec(memory_space=pltpu.VMEM)
    return pl.pallas_call(
        residual_kernel,
        out_shape=jax.ShapeDtypeStruct(parts.shape, jnp.bfloat16),
        in_specs=[vmem] + [ANY] * len(after),
        out_specs=vmem,
        compiler_params=pltpu.CompilerParams(vmem_limit_bytes=48 * 2**20),
        cost_estimate=pl.CostEstimate(flops=parts.size, bytes_accessed=4 * parts.size, transcendentals=0),
    )(parts, *after)


def order_kernel(*refs):
    pass


def mark_kernel(*refs):
    refs[-1][...] = jnp.zeros(refs[-1].shape, jnp.float32)


def mark(arrays, us):
    return pl.pallas_call(
        mark_kernel,
        out_shape=jax.ShapeDtypeStruct((8, 128), jnp.float32),
        in_specs=[ANY] * len(arrays),
        out_specs=pl.BlockSpec(memory_space=pltpu.VMEM),
        cost_estimate=pl.CostEstimate(flops=int(us * 10**9), bytes_accessed=1, transcendentals=0),
    )(*arrays)


def in_order(array, before):
    return pl.pallas_call(
        order_kernel,
        out_shape=jax.ShapeDtypeStruct(array.shape, array.dtype),
        in_specs=[ANY, ANY],
        out_specs=ANY,
        input_output_aliases={0: 0},
        cost_estimate=pl.CostEstimate(flops=1, bytes_accessed=1, transcendentals=0),
    )(array, before)


def step_kernel(factor, wants, info, ht_ref, rt_ref, m_ref, keep_ref, code_ref, *refs):
    want_state, want_coeffs = wants
    if want_coeffs:
        mine_ref, other_ref = refs[-2:]
        mine = mine_ref.shape[0]
    if want_state:
        new_ref = refs[-3 if want_coeffs else -1]
    rows = m_ref.shape[0]
    width = m_ref.shape[1]
    rt = rt_ref[...].reshape(width, rt_ref.shape[2])
    keep = keep_ref[0]
    code = code_ref[0]
    for start in range(0, rows, TILE):
        size = min(TILE, rows - start)
        f = pl.ds(start, size)
        grad = lax.dot_general(
            ht_ref[f, :], rt, (((1,), (1,)), ((), ())), preferred_element_type=jnp.float32
        )
        primed = DECAY * m_ref[f, :].astype(jnp.float32) + grad * factor
        low = primed.astype(jnp.bfloat16)
        for a in range(0, width if want_state else 0, 256):
            b = min(a + 256, width)
            gone = jnp.dot(low[:, a:b], keep[a:b, a:b], preferred_element_type=jnp.float32)
            new_ref[f, a:b] = (primed[:, a:b] - gone).astype(jnp.bfloat16)
        if want_coeffs:
            coeffs = lax.dot_general(
                code, low, (((1,), (1,)), ((), ())), preferred_element_type=jnp.float32
            ).astype(jnp.bfloat16)
            mine_ref[:, f] = coeffs[:mine]
            other_ref[:, f] = coeffs[mine:]


def momentum_step(chips, ht, rt, momentum, keep, code, factor, wants, before):
    n = chips.shape[0]
    n_chips = code.shape[0]
    rows, width_all = momentum.shape
    tokens = ht.shape[1]
    shards, _, slab, _ = rt.shape
    width = shards * slab
    kept = code.shape[1]
    mine = kept // 2
    in_specs = [
        pl.BlockSpec((rows, tokens), lambda u, c: (0, 0)),
        pl.BlockSpec((shards, None, slab, tokens), lambda u, c: (0, u, 0, 0)),
        pl.BlockSpec((rows, width), lambda u, c: (0, c[u])),
        pl.BlockSpec((1, width, width), lambda u, c: (c[u], 0, 0)),
        pl.BlockSpec((1, kept, width), lambda u, c: (c[u], 0, 0)),
    ]
    args = [ht, rt, momentum, keep, code]
    alias = {6 + i: i for i in range(len(before))}
    in_specs += [ANY] * len(before)
    args += before
    want_state, want_coeffs = wants
    state_shape = jax.ShapeDtypeStruct((rows, width_all), jnp.bfloat16)
    state_spec = pl.BlockSpec((rows, width), lambda u, c: (0, c[u]))
    coeff_shape = jax.ShapeDtypeStruct((n_chips, mine, rows), jnp.bfloat16)
    coeff_spec = pl.BlockSpec((None, mine, rows), lambda u, c: (c[u], 0, 0))
    return pl.pallas_call(
        functools.partial(step_kernel, factor, wants),
        out_shape=(state_shape,) * want_state + (coeff_shape,) * (2 * want_coeffs),
        grid_spec=pltpu.PrefetchScalarGridSpec(
            num_scalar_prefetch=1,
            grid=(n,),
            in_specs=in_specs,
            out_specs=(state_spec,) * want_state + (coeff_spec,) * (2 * want_coeffs),
        ),
        input_output_aliases=alias,
        compiler_params=pltpu.CompilerParams(
            vmem_limit_bytes=62 * 2**20, dimension_semantics=("arbitrary",)
        ),
        cost_estimate=pl.CostEstimate(
            flops=2 * n * rows * width * (tokens + 256 + kept),
            bytes_accessed=2 * (2 * n * rows * width + rows * tokens),
            transcendentals=0,
        ),
    )(chips, *args)


def table_kernel(info, freqs_ref, cosines_ref, keep_ref, code_ref):
    rows, width = code_ref.shape[1:]
    per = width // CL
    kept = rows // per
    freqs = freqs_ref[0]
    onehot = (freqs == lax.broadcasted_iota(jnp.int32, (rows, CL), 1)).astype(jnp.float32)
    chosen = jnp.dot(
        onehot, cosines_ref[...], precision=lax.Precision.HIGHEST, preferred_element_type=jnp.float32
    )
    wide = jnp.concatenate([chosen] * per, axis=1)
    block = lax.broadcasted_iota(jnp.int32, (rows, width), 0) // kept + info[0] * (per // 2)
    block = jnp.where(block >= per, block - per, block)
    wide = jnp.where(block == lax.broadcasted_iota(jnp.int32, (rows, width), 1) // CL, wide, 0.0)
    code_ref[0] = wide.astype(jnp.bfloat16)
    keep_ref[...] = jnp.zeros(keep_ref.shape, jnp.bfloat16)
    for a in range(0, width, 128):
        tile = wide[:, a : a + 128]
        keep_ref[0, a : a + 128, a : a + 128] = lax.dot_general(
            tile,
            tile,
            (((0,), (0,)), ((), ())),
            precision=lax.Precision.HIGHEST,
            preferred_element_type=jnp.float32,
        ).astype(jnp.bfloat16)


def tables(freqs, core, n_chips):
    blocks, kept = freqs.shape
    per = blocks // n_chips
    ordered = freqs.reshape(n_chips, 2, per // 2 * kept)
    ordered = jnp.where(core == 0, ordered, ordered[:, ::-1]).reshape(n_chips, per * kept, 1)
    return pl.pallas_call(
        table_kernel,
        out_shape=(
            jax.ShapeDtypeStruct((n_chips, per * CL, per * CL), jnp.bfloat16),
            jax.ShapeDtypeStruct((n_chips, per * kept, per * CL), jnp.bfloat16),
        ),
        grid=(n_chips,),
        in_specs=[
            pl.BlockSpec(memory_space=pltpu.SMEM),
            pl.BlockSpec((1, per * kept, 1), lambda u: (u, 0, 0)),
            pl.BlockSpec((CL, CL), lambda u: (0, 0)),
        ],
        out_specs=(
            pl.BlockSpec((1, per * CL, per * CL), lambda u: (u, 0, 0)),
            pl.BlockSpec((1, per * kept, per * CL), lambda u: (u, 0, 0)),
        ),
        compiler_params=pltpu.CompilerParams(vmem_limit_bytes=32 * 2**20),
        cost_estimate=pl.CostEstimate(flops=10**9, bytes_accessed=4 * 10**6, transcendentals=0),
    )(core[None].astype(jnp.int32), ordered, cosine_table())


def per_device(sizes, hidden, weight, momentum, target, freqs):
    send = lambda v, **by: lax.ppermute(v, AXES, shift(sizes, **by))
    zh, x, c = (lax.axis_index(a) for a in DP)
    n_zh, n_x = sizes[0], sizes[1]
    n_tensor = sizes[3] * sizes[4]
    shard = lax.axis_index(TENSOR)
    n_chips = n_zh * n_x
    ht = hidden.T
    own = weight.T
    factor = 1.0 / math.sqrt(hidden.shape[0])

    cut = own.shape[0] // 2
    blocks = {(0, 0): [own], (1, 0): [send(own, zh=1)], (0, 1): [send(own, x=-1)], (0, 3): [send(own, x=1)]}
    for z in range(2):
        if z:
            blocks[z, 1] = [send(blocks[z, 0][0], x=-1)]
            blocks[z, 3] = [send(blocks[z, 0][0], x=1)]
        blocks[z, 2] = [send(blocks[z, 1][0][:cut], x=-1), send(blocks[z, 3][0][cut:], x=1)]
    swapped = {s: [send(piece, c=1) for piece in b] for s, b in blocks.items()}
    keep, code = tables(freqs, c, n_chips)

    core = c[None].astype(jnp.int32)
    chips, partials = [], []
    for chunk, us in zip(CHUNKS, CHUNK_US):
        at = jnp.stack([((zh + s[0]) % n_zh) * n_x + (x + s[1]) % n_x for s in chunk]).astype(jnp.int32)
        chips.append(at)
        info = jnp.concatenate([core, (at == shard).astype(jnp.int32)])
        pairs = [b for s in chunk for b in (blocks[s], swapped[s])]
        partials.append(partial_output(n_tensor, info, ht, target, pairs, us))
    rest = [piece for s in CHUNKS[1] for piece in swapped[s]]
    first = residual_copies(lax.all_to_all(partials[0], TENSOR, 0, 0), [mark(rest, MARK_US)])
    first = lax.all_to_all(first, TENSOR, 0, 0)
    last = residual_copies(lax.all_to_all(in_order(partials[1], first), TENSOR, 0, 0), [])
    gathered = [first, lax.all_to_all(last, TENSOR, 0, 0)]

    step = lambda k, *how: momentum_step(chips[k], ht, gathered[k], momentum[0], keep, code, factor, *how)
    state, mine, other = step(0, (True, True), [])
    mine, other = step(1, (False, True), [mine, other])
    (state,) = step(1, (True, False), [state])

    pair = (mine.astype(jnp.float32) + send(other, c=1).astype(jnp.float32)).astype(jnp.bfloat16)
    total = jnp.sum(lax.all_to_all(pair, ("zh", "x"), 0, 0).astype(jnp.float32), axis=0)
    n_dp = n_chips * sizes[2]
    per = freqs.shape[0] // n_dp
    own_freqs = lax.dynamic_slice_in_dim(freqs, lax.axis_index(DP) * per, per, 0)
    onehot = (own_freqs[:, :, None] == jnp.arange(CL, dtype=jnp.int32)).astype(jnp.float32)
    own_basis = jnp.einsum("ckv,vj->ckj", onehot, cosine_table(), precision=lax.Precision.HIGHEST)
    decoded = jnp.einsum(
        "ckf,ckj->cjf",
        total.reshape(per, total.shape[0] // per, total.shape[1]),
        own_basis * (1.0 / n_dp),
        precision=lax.Precision.HIGHEST,
    )
    return state[None], decoded.reshape(per * CL, -1).T


def solution(mesh):
    sizes = (2, 4, 2, 2, 4)
    fine = Mesh(mesh.devices.reshape(sizes), AXES)
    in_specs = (P(DP, TENSOR), P(TENSOR, DP), P(DP, TENSOR, None), P(DP, TENSOR), P())
    out_specs = (P(DP, TENSOR, None), P(TENSOR, DP))
    return jax.shard_map(
        functools.partial(per_device, sizes),
        mesh=fine,
        in_specs=in_specs,
        out_specs=out_specs,
        check_vma=False,
    )
```

```python
import functools
import math

import jax
import jax.numpy as jnp
from jax import lax
from jax.experimental import pallas as pl
from jax.experimental.pallas import tpu as pltpu
from jax.sharding import Mesh, PartitionSpec as P
import numpy as np

CL = 64
DECAY = 0.9
AXES = ("zh", "x", "c", "zl", "y")
DP = ("zh", "x", "c")
TENSOR = ("zl", "y")
ANY = pl.BlockSpec(memory_space=pl.ANY)
TILE = 896
CHUNKS = (((0, 0), (1, 0), (0, 1), (0, 3)), ((0, 2), (1, 1), (1, 3), (1, 2)))
CHUNK_US = (4, 6)
MARK_US = 6


def cosine_table():
    freq_ids = jnp.arange(CL, dtype=jnp.float32)[:, None]
    cell_ids = jnp.arange(CL, dtype=jnp.float32)[None, :]
    scale_row = jnp.where(freq_ids == 0, math.sqrt(1.0 / CL), math.sqrt(2.0 / CL))
    return scale_row * jnp.cos(math.pi * (2.0 * cell_ids + 1.0) * freq_ids / (2.0 * CL))


def shift(sizes, **by):
    step = [by.get(a, 0) for a in AXES]
    pairs = []
    for at in np.ndindex(*sizes):
        to = [(a + s) % n for a, s, n in zip(at, step, sizes)]
        pairs.append((int(np.ravel_multi_index(at, sizes)), int(np.ravel_multi_index(to, sizes))))
    return pairs


def output_kernel(pieces, info, ht_ref, target_ref, *refs):
    blocks, (out_ref, w_ref, sems) = refs[: sum(pieces)], refs[-3:]
    core = info[0]
    shards, n, rows, _ = out_ref.shape
    half = shards * rows // 2
    copies = []
    at = 0
    for k, count in enumerate(pieces):
        slot = core if k % 2 == 0 else 1 - core
        base = (k // 2 * 2 + slot) * half
        for _ in range(count):
            size = blocks[at].shape[0]
            to = pl.ds(pl.multiple_of(base, 16), size)
            copies.append((k // 2, pltpu.make_async_copy(blocks[at], w_ref.at[to], sems.at[at])))
            base = base + size
            at += 1
    for _, copy in copies:
        copy.start()
    for u in range(n):
        for unit, copy in copies:
            if unit == u:
                copy.wait()
        value = jnp.dot(
            w_ref[2 * u * half : 2 * (u + 1) * half], ht_ref[...], preferred_element_type=jnp.float32
        )
        for i in range(shards):
            out_ref[i, u] = value[i * rows : (i + 1) * rows].astype(jnp.bfloat16)

        @pl.when(info[1 + u] != 0)
        def _():
            goal = target_ref[...].astype(jnp.float32).T
            for i in range(shards):
                here = out_ref[i, u].astype(jnp.float32) - goal[i * rows : (i + 1) * rows]
                out_ref[i, u] = here.astype(jnp.bfloat16)


def partial_output(shards, info, ht, target, blocks, us):
    depth, count = ht.shape
    width = target.shape[1]
    n = len(blocks) // 2
    pieces = tuple(len(b) for b in blocks)
    blocks = [piece for b in blocks for piece in b]
    vmem = pl.BlockSpec(memory_space=pltpu.VMEM)
    return pl.pallas_call(
        functools.partial(output_kernel, pieces),
        out_shape=jax.ShapeDtypeStruct((shards, n, width // shards, count), jnp.bfloat16),
        in_specs=[pl.BlockSpec(memory_space=pltpu.SMEM), vmem, vmem] + [ANY] * len(blocks),
        out_specs=vmem,
        scratch_shapes=[
            pltpu.VMEM((n * width, depth), jnp.bfloat16),
            pltpu.SemaphoreType.DMA((len(blocks),)),
        ],
        compiler_params=pltpu.CompilerParams(vmem_limit_bytes=56 * 2**20),
        cost_estimate=pl.CostEstimate(flops=int(us * 10**9), bytes_accessed=1, transcendentals=0),
    )(info, ht, target, *blocks)


def residual_kernel(parts_ref, *refs):
    out_ref = refs[-1]
    for u in range(out_ref.shape[1]):
        total = jnp.sum(parts_ref[:, u].astype(jnp.float32), axis=0).astype(jnp.bfloat16)
        for k in range(out_ref.shape[0]):
            out_ref[k, u] = total


def residual_copies(parts, after):
    vmem = pl.BlockSpec(memory_space=pltpu.VMEM)
    return pl.pallas_call(
        residual_kernel,
        out_shape=jax.ShapeDtypeStruct(parts.shape, jnp.bfloat16),
        in_specs=[vmem] + [ANY] * len(after),
        out_specs=vmem,
        compiler_params=pltpu.CompilerParams(vmem_limit_bytes=48 * 2**20),
        cost_estimate=pl.CostEstimate(flops=parts.size, bytes_accessed=4 * parts.size, transcendentals=0),
    )(parts, *after)


def order_kernel(*refs):
    pass


def mark_kernel(*refs):
    refs[-1][...] = jnp.zeros(refs[-1].shape, jnp.float32)


def mark(arrays, us):
    return pl.pallas_call(
        mark_kernel,
        out_shape=jax.ShapeDtypeStruct((8, 128), jnp.float32),
        in_specs=[ANY] * len(arrays),
        out_specs=pl.BlockSpec(memory_space=pltpu.VMEM),
        cost_estimate=pl.CostEstimate(flops=int(us * 10**9), bytes_accessed=1, transcendentals=0),
    )(*arrays)


def in_order(array, before):
    return pl.pallas_call(
        order_kernel,
        out_shape=jax.ShapeDtypeStruct(array.shape, array.dtype),
        in_specs=[ANY, ANY],
        out_specs=ANY,
        input_output_aliases={0: 0},
        cost_estimate=pl.CostEstimate(flops=1, bytes_accessed=1, transcendentals=0),
    )(array, before)


def step_kernel(factor, wants, info, ht_ref, rt_ref, m_ref, keep_ref, code_ref, *refs):
    want_state, want_coeffs = wants
    if want_coeffs:
        mine_ref, other_ref = refs[-2:]
        mine = mine_ref.shape[0]
    if want_state:
        new_ref = refs[-3 if want_coeffs else -1]
    rows = m_ref.shape[0]
    width = m_ref.shape[1]
    rt = rt_ref[...].reshape(width, rt_ref.shape[2])
    keep = keep_ref[0]
    code = code_ref[0]
    for start in range(0, rows, TILE):
        size = min(TILE, rows - start)
        f = pl.ds(start, size)
        grad = lax.dot_general(
            ht_ref[f, :], rt, (((1,), (1,)), ((), ())), preferred_element_type=jnp.float32
        )
        primed = DECAY * m_ref[f, :].astype(jnp.float32) + grad * factor
        low = primed.astype(jnp.bfloat16)
        for a in range(0, width if want_state else 0, 256):
            b = min(a + 256, width)
            gone = jnp.dot(low[:, a:b], keep[a:b, a:b], preferred_element_type=jnp.float32)
            new_ref[f, a:b] = (primed[:, a:b] - gone).astype(jnp.bfloat16)
        if want_coeffs:
            coeffs = lax.dot_general(
                code, low, (((1,), (1,)), ((), ())), preferred_element_type=jnp.float32
            ).astype(jnp.bfloat16)
            mine_ref[:, f] = coeffs[:mine]
            other_ref[:, f] = coeffs[mine:]


def momentum_step(chips, ht, rt, momentum, keep, code, factor, wants, before):
    n = chips.shape[0]
    n_chips = code.shape[0]
    rows, width_all = momentum.shape
    tokens = ht.shape[1]
    shards, _, slab, _ = rt.shape
    width = shards * slab
    kept = code.shape[1]
    mine = kept // 2
    in_specs = [
        pl.BlockSpec((rows, tokens), lambda u, c: (0, 0)),
        pl.BlockSpec((shards, None, slab, tokens), lambda u, c: (0, u, 0, 0)),
        pl.BlockSpec((rows, width), lambda u, c: (0, c[u])),
        pl.BlockSpec((1, width, width), lambda u, c: (c[u], 0, 0)),
        pl.BlockSpec((1, kept, width), lambda u, c: (c[u], 0, 0)),
    ]
    args = [ht, rt, momentum, keep, code]
    alias = {6 + i: i for i in range(len(before))}
    in_specs += [ANY] * len(before)
    args += before
    want_state, want_coeffs = wants
    state_shape = jax.ShapeDtypeStruct((rows, width_all), jnp.bfloat16)
    state_spec = pl.BlockSpec((rows, width), lambda u, c: (0, c[u]))
    coeff_shape = jax.ShapeDtypeStruct((n_chips, mine, rows), jnp.bfloat16)
    coeff_spec = pl.BlockSpec((None, mine, rows), lambda u, c: (c[u], 0, 0))
    return pl.pallas_call(
        functools.partial(step_kernel, factor, wants),
        out_shape=(state_shape,) * want_state + (coeff_shape,) * (2 * want_coeffs),
        grid_spec=pltpu.PrefetchScalarGridSpec(
            num_scalar_prefetch=1,
            grid=(n,),
            in_specs=in_specs,
            out_specs=(state_spec,) * want_state + (coeff_spec,) * (2 * want_coeffs),
        ),
        input_output_aliases=alias,
        compiler_params=pltpu.CompilerParams(
            vmem_limit_bytes=62 * 2**20, dimension_semantics=("arbitrary",)
        ),
        cost_estimate=pl.CostEstimate(
            flops=2 * n * rows * width * (tokens + 256 + kept),
            bytes_accessed=2 * (2 * n * rows * width + rows * tokens),
            transcendentals=0,
        ),
    )(chips, *args)


def table_kernel(info, freqs_ref, cosines_ref, keep_ref, code_ref):
    rows, width = code_ref.shape[1:]
    per = width // CL
    kept = rows // per
    freqs = freqs_ref[0]
    onehot = (freqs == lax.broadcasted_iota(jnp.int32, (rows, CL), 1)).astype(jnp.float32)
    chosen = jnp.dot(
        onehot, cosines_ref[...], precision=lax.Precision.HIGHEST, preferred_element_type=jnp.float32
    )
    wide = jnp.concatenate([chosen] * per, axis=1)
    block = lax.broadcasted_iota(jnp.int32, (rows, width), 0) // kept + info[0] * (per // 2)
    block = jnp.where(block >= per, block - per, block)
    wide = jnp.where(block == lax.broadcasted_iota(jnp.int32, (rows, width), 1) // CL, wide, 0.0)
    code_ref[0] = wide.astype(jnp.bfloat16)
    keep_ref[...] = jnp.zeros(keep_ref.shape, jnp.bfloat16)
    for a in range(0, width, 128):
        tile = wide[:, a : a + 128]
        keep_ref[0, a : a + 128, a : a + 128] = lax.dot_general(
            tile,
            tile,
            (((0,), (0,)), ((), ())),
            precision=lax.Precision.HIGHEST,
            preferred_element_type=jnp.float32,
        ).astype(jnp.bfloat16)


def tables(freqs, core, n_chips):
    blocks, kept = freqs.shape
    per = blocks // n_chips
    ordered = freqs.reshape(n_chips, 2, per // 2 * kept)
    ordered = jnp.where(core == 0, ordered, ordered[:, ::-1]).reshape(n_chips, per * kept, 1)
    return pl.pallas_call(
        table_kernel,
        out_shape=(
            jax.ShapeDtypeStruct((n_chips, per * CL, per * CL), jnp.bfloat16),
            jax.ShapeDtypeStruct((n_chips, per * kept, per * CL), jnp.bfloat16),
        ),
        grid=(n_chips,),
        in_specs=[
            pl.BlockSpec(memory_space=pltpu.SMEM),
            pl.BlockSpec((1, per * kept, 1), lambda u: (u, 0, 0)),
            pl.BlockSpec((CL, CL), lambda u: (0, 0)),
        ],
        out_specs=(
            pl.BlockSpec((1, per * CL, per * CL), lambda u: (u, 0, 0)),
            pl.BlockSpec((1, per * kept, per * CL), lambda u: (u, 0, 0)),
        ),
        compiler_params=pltpu.CompilerParams(vmem_limit_bytes=32 * 2**20),
        cost_estimate=pl.CostEstimate(flops=10**9, bytes_accessed=4 * 10**6, transcendentals=0),
    )(core[None].astype(jnp.int32), ordered, cosine_table())


def per_device(sizes, hidden, weight, momentum, target, freqs):
    send = lambda v, **by: lax.ppermute(v, AXES, shift(sizes, **by))
    zh, x, c = (lax.axis_index(a) for a in DP)
    n_zh, n_x = sizes[0], sizes[1]
    n_tensor = sizes[3] * sizes[4]
    shard = lax.axis_index(TENSOR)
    n_chips = n_zh * n_x
    ht = hidden.T
    own = weight.T
    factor = 1.0 / math.sqrt(hidden.shape[0])

    cut = own.shape[0] // 2
    blocks = {(0, 0): [own], (1, 0): [send(own, zh=1)], (0, 1): [send(own, x=-1)], (0, 3): [send(own, x=1)]}
    blocks[0, 2] = [send(blocks[0, 1][0][:cut], x=-1), send(blocks[0, 3][0][cut:], x=1)]
    halves = (blocks[1, 0][0][:cut], blocks[1, 0][0][cut:])
    blocks[1, 1] = [send(h, x=-1) for h in halves]
    blocks[1, 3] = [send(h, x=1) for h in halves]
    blocks[1, 2] = [send(blocks[1, 1][0], x=-1), send(blocks[1, 3][1], x=1)]
    swapped = {s: [send(piece, c=1) for piece in b] for s, b in blocks.items()}
    keep, code = tables(freqs, c, n_chips)

    core = c[None].astype(jnp.int32)
    chips, partials = [], []
    for chunk, us in zip(CHUNKS, CHUNK_US):
        at = jnp.stack([((zh + s[0]) % n_zh) * n_x + (x + s[1]) % n_x for s in chunk]).astype(jnp.int32)
        chips.append(at)
        info = jnp.concatenate([core, (at == shard).astype(jnp.int32)])
        pairs = [b for s in chunk for b in (blocks[s], swapped[s])]
        partials.append(partial_output(n_tensor, info, ht, target, pairs, us))
    rest = [piece for s in CHUNKS[1] for piece in swapped[s]]
    first = residual_copies(lax.all_to_all(partials[0], TENSOR, 0, 0), [mark(rest, MARK_US)])
    first = lax.all_to_all(first, TENSOR, 0, 0)
    last = residual_copies(lax.all_to_all(in_order(partials[1], first), TENSOR, 0, 0), [])
    gathered = [first, lax.all_to_all(last, TENSOR, 0, 0)]

    step = lambda k, *how: momentum_step(chips[k], ht, gathered[k], momentum[0], keep, code, factor, *how)
    state, mine, other = step(0, (True, True), [])
    mine, other = step(1, (False, True), [mine, other])
    (state,) = step(1, (True, False), [state])

    pair = (mine.astype(jnp.float32) + send(other, c=1).astype(jnp.float32)).astype(jnp.bfloat16)
    total = jnp.sum(lax.all_to_all(pair, ("zh", "x"), 0, 0).astype(jnp.float32), axis=0)
    n_dp = n_chips * sizes[2]
    per = freqs.shape[0] // n_dp
    own_freqs = lax.dynamic_slice_in_dim(freqs, lax.axis_index(DP) * per, per, 0)
    onehot = (own_freqs[:, :, None] == jnp.arange(CL, dtype=jnp.int32)).astype(jnp.float32)
    own_basis = jnp.einsum("ckv,vj->ckj", onehot, cosine_table(), precision=lax.Precision.HIGHEST)
    decoded = jnp.einsum(
        "ckf,ckj->cjf",
        total.reshape(per, total.shape[0] // per, total.shape[1]),
        own_basis * (1.0 / n_dp),
        precision=lax.Precision.HIGHEST,
    )
    return state[None], decoded.reshape(per * CL, -1).T


def solution(mesh):
    sizes = (2, 4, 2, 2, 4)
    fine = Mesh(mesh.devices.reshape(sizes), AXES)
    in_specs = (P(DP, TENSOR), P(TENSOR, DP), P(DP, TENSOR, None), P(DP, TENSOR), P())
    out_specs = (P(DP, TENSOR, None), P(TENSOR, DP))
    return jax.shard_map(
        functools.partial(per_device, sizes),
        mesh=fine,
        in_specs=in_specs,
        out_specs=out_specs,
        check_vma=False,
    )
```
